32 devices in a mesh: fsdp: 8 (over y, x, core), ep: 4 (over z).
Axes of the slice: x: 2, y: 2, z: 4, core: 2. Of those that a mesh axis runs over, the one named last changes fastest.
Arguments:
- expert_ids: int32 [128, 4], P('ep'), may hold values from 0 to 15, all different within a row; in each aligned block of 32 rows (0 to 31, 32 to 63, ...) at most 16 rows name the same one
- route_weights: float32 [128, 4], P('ep'), may hold values from 0.1 to 1
- residual_grad: bfloat16 [128, 6144], P('ep', 'fsdp'), may hold values from -6 to 6
- hidden_grad: bfloat16 [32, 64, 2688], P('ep'), may hold values from -6 to 6
- gate_pre: bfloat16 [32, 64, 2688], P('ep'), may hold values from -6 to 6
- up_pre: bfloat16 [32, 64, 2688], P('ep'), may hold values from -6 to 6
- gate_weight: bfloat16 [32, 6144, 2688], P('ep', 'fsdp'), may hold values from -0.0625 to 0.0625
- up_weight: bfloat16 [32, 6144, 2688], P('ep', 'fsdp'), may hold values from -0.0625 to 0.0625
- attn_context: bfloat16 [2048, 6144], P('fsdp', 'ep'), may hold values from -6 to 6
- attn_grad: bfloat16 [2048, 6144], P('fsdp'), may hold values from -6 to 6
Outputs:
- input_grad: bfloat16 [128, 6144], P('ep', 'fsdp')
- proj_weight_grad: float32 [6144, 6144], P('ep', 'fsdp')
The draws below stay inside these ranges and needn't reach their ends.
Inputs may be any that keep to these rules, and one draw needn't show every extreme that they name: `expert_ids`: each row names 4 different experts. Among the rows of one ep index no expert is named more than 16 times, a bound that some block reaches.
All inputs are finite; a program needn't handle non-finite values.
Results may differ from the reference program's by a relative error of at most 0.005.
Values may be sent and summed in bfloat16 or wider, within the bound.
A program may use at most 192 MiB of HBM per device.

```python
import math
import jax
import jax.numpy as jnp
import numpy as np
from jax import lax

D = 6144
FF = 10752
EXPERTS = 16
TOP = 4
CAP = 16
TOK_DEV = 32
HALF = 2688
SLOTS = 64
TOKENS = 128
ATT_TOKENS = 2048
N_EP = 4


def with_spikes(result, own_key, source, target, blocks, factor):
    owner, partner = [(jnp.arange(result.shape[axis_at]) // (result.shape[axis_at] // blocks)).reshape([-1 if axis == axis_at else 1 for axis in range(result.ndim)]) for axis_at in (source, target)]
    chosen = jax.random.permutation(own_key, blocks)[partner]
    strong = (owner == chosen) | (owner == (partner + blocks // 2) % blocks)
    return jnp.where(strong, factor * result, result)


def steps_of(key, shape, split, smallest, top_value):
    level, own = 1.0, jax.random.fold_in(key, 6)
    for position, blocks in split:
        draws = jnp.exp(jax.random.uniform(jax.random.fold_in(own, position), (blocks,), jnp.float32, smallest / len(split), top_value / len(split)))
        level = level * jnp.repeat(draws, shape[position] // blocks).reshape([-1 if axis == position else 1 for axis in range(len(shape))])
    return level


def routed_block(stream_key, own, number, rows, count, top, reach, slope):
    order = jax.random.permutation(stream_key, count)
    crowded, usual = portions_of(count, rows * top, reach, slope, True), portions_of(count, rows * top, reach, slope, False)
    places = jnp.arange(count)

    def named(lengths, offset_by):
        used = int((lengths > 0).sum())
        fixed = max(1, used // 4)
        shifted = fixed + (places - fixed + offset_by * (used - fixed)) % max(1, count - fixed)
        return jnp.zeros((count,), jnp.int32).at[order[jnp.where(places < fixed, places, shifted)]].set(jnp.asarray(lengths, jnp.int32))

    lengths = jnp.where(number % 4 == 0, named(crowded, number // 4), named(usual, number - number // 4 - 1))
    mixed = jax.random.permutation(jax.random.fold_in(own, 3), count)
    donor, receiver = mixed[0:count // 2 * 2:2], mixed[1:count // 2 * 2:2]
    margin = jnp.minimum(lengths[donor] - 1, reach - lengths[receiver]) // 2
    margin = jnp.where((donor == order[0]) | (receiver == order[0]) | (lengths[receiver] == 0), 0, jnp.maximum(margin, 0))
    shifted = jax.random.randint(jax.random.fold_in(own, 4), (count // 2,), 0, 1 << 20) % (margin + 1)
    lengths = lengths.at[donor].add(-shifted).at[receiver].add(shifted)
    labels = jnp.searchsorted(jnp.cumsum(lengths), jnp.arange(rows * top), side="right").astype(jnp.int32)
    listing = labels.reshape(top, rows).T
    listing = listing[jax.random.permutation(jax.random.fold_in(own, 1), rows)]
    offset_by = jax.random.randint(jax.random.fold_in(own, 2), (rows, 1), 0, top)
    return jnp.take_along_axis(listing, (jnp.arange(top)[None, :] + offset_by) % top, axis=1)


def portions_of(amount, total, reach, skew, full):
    weights = [(1 << 20) // math.isqrt(grade ** skew) + 1 for grade in range(1, amount + 1)]
    largest = reach if full else min(reach, max(-(-total // amount), total * weights[0] // sum(weights)))
    least = 1 if total - largest >= amount - 1 else 0
    given, surplus = [largest] + [least] * (amount - 1), total - largest - least * (amount - 1)
    while surplus > 0:
        free = [i for i in range(1, amount) if given[i] < largest] or [i for i in range(1, amount) if given[i] < reach]
        whole, remaining = sum([weights[i] for i in free]), surplus
        for i in free:
            more = min(reach - given[i], max(1, remaining * weights[i] // whole), surplus)
            given[i] = given[i] + more
            surplus = surplus - more
    return np.array(given)


def scatter_about(stream_key, shape, width, bound, split=(), kind=jnp.bfloat16):
    result = jax.random.normal(stream_key, shape, jnp.float32) * width
    if len(split) > 0:
        result = steps_of(stream_key, shape, split, -0.22, 0.18) * result
    return jnp.clip(result, min=-bound, max=bound).astype(kind)


def noise_with(rng, extent, scale, most, split, heavy, kind=jnp.bfloat16):
    array = scale * jax.random.normal(rng, extent, jnp.float32)
    if split:
        array = array * steps_of(rng, extent, split, -0.22, 0.18)
    return jnp.clip(with_spikes(array, jax.random.fold_in(rng, 3), *heavy), -most, most).astype(kind)


def setup_inputs(seed: int = 0) -> dict:
    key_list = jax.random.split(jax.random.key(seed), 11)
    expert_ids_keys = jax.random.split(jax.random.fold_in(key_list[0], 1), TOKENS // TOK_DEV)
    expert_ids_turns = jax.random.permutation(jax.random.fold_in(key_list[0], 3), TOKENS // TOK_DEV)
    expert_ids = jax.vmap(lambda own, number: routed_block(jax.random.fold_in(key_list[0], 2), own, number, TOK_DEV, EXPERTS, TOP, CAP, 2))(expert_ids_keys, expert_ids_turns).reshape((TOKENS, TOP))
    route_weights = jnp.clip(jnp.exp(math.log(1.0) - 2.3025851 * jax.random.uniform(key_list[1], (TOKENS, TOP), jnp.float32) ** steps_of(key_list[1], (TOKENS, TOP), ((0, 4),), -0.2, 0.2)), 0.1, 1.0)
    residual_grad = scatter_about(key_list[2], (TOKENS, D), 1.0, 6.0, ((0, 4), (1, 8)))
    hidden_grad = scatter_about(key_list[3], (2 * EXPERTS, SLOTS, HALF), 1.0, 6.0, ((0, 4),))
    gate_pre = scatter_about(key_list[4], (2 * EXPERTS, SLOTS, HALF), 1.5, 6.0, ((0, 4),))
    up_pre = scatter_about(key_list[5], (2 * EXPERTS, SLOTS, HALF), 1.0, 6.0, ((0, 4),))
    gate_weight = scatter_about(key_list[6], (2 * EXPERTS, D, HALF), FF ** -0.5, 0.0625, ((0, 4), (1, 8)))
    up_weight = scatter_about(key_list[7], (2 * EXPERTS, D, HALF), FF ** -0.5, 0.0625, ((0, 4), (1, 8)))
    attn_context = scatter_about(key_list[8], (ATT_TOKENS, D), 1.0, 6.0, ((0, 8), (1, 4)))
    attn_grad = noise_with(key_list[9], (ATT_TOKENS, D), 1.0, 6.0, ((0, 8),), (0, 1, 8, 2.0))
    return dict(expert_ids=expert_ids, route_weights=route_weights, residual_grad=residual_grad, hidden_grad=hidden_grad, gate_pre=gate_pre, up_pre=up_pre, gate_weight=gate_weight, up_weight=up_weight, attn_context=attn_context, attn_grad=attn_grad)


def slot_table(expert_ids):
    flat = expert_ids.reshape(N_EP, TOK_DEV * TOP)
    onehot = (flat[:, :, None] == jnp.arange(EXPERTS, dtype=jnp.int32)[None, None, :]).astype(jnp.int32)
    before = jnp.cumsum(onehot, axis=1) - onehot
    return jnp.sum(before * onehot, axis=2).reshape(N_EP, TOK_DEV, TOP).astype(jnp.int32)


def reference(expert_ids, route_weights, residual_grad, hidden_grad, gate_pre, up_pre, gate_weight, up_weight, attn_context, attn_grad):
    gate = gate_pre.astype(jnp.float32)
    upper = up_pre.astype(jnp.float32)
    grads = hidden_grad.astype(jnp.float32)
    sig = jax.nn.sigmoid(gate)
    up_term = (grads * gate * sig).astype(jnp.bfloat16)
    gate_term = (grads * upper * sig * (1.0 + gate * (1.0 - sig))).astype(jnp.bfloat16)

    def one_block(items):
        gterm, uterm, gweight, uweight = items
        first = jnp.dot(gterm, gweight.T, preferred_element_type=jnp.float32)
        second = jnp.dot(uterm, uweight.T, preferred_element_type=jnp.float32)
        return (first + second).astype(jnp.bfloat16)

    expert_rows = lax.map(one_block, (gate_term, up_term, gate_weight, up_weight))
    table = expert_rows.astype(jnp.float32).reshape(2 * EXPERTS, N_EP, CAP, D)
    slots = slot_table(expert_ids)
    ids = expert_ids.reshape(N_EP, TOK_DEV, TOP)
    source = jnp.arange(N_EP, dtype=jnp.int32)[:, None, None]
    low_half = table[2 * ids, source, slots]
    high_half = table[2 * ids + 1, source, slots]
    weights = route_weights.reshape(N_EP, TOK_DEV, TOP, 1)
    combined = jnp.sum(weights * (low_half + high_half), axis=2).reshape(TOKENS, D)
    input_grad = (residual_grad.astype(jnp.float32) + combined).astype(jnp.bfloat16)
    proj_weight_grad = jnp.dot(attn_context.T, attn_grad, preferred_element_type=jnp.float32)
    return input_grad, proj_weight_grad
```

```python
import functools

import jax
import jax.numpy as jnp
from jax import lax
from jax.experimental import pallas as pl
from jax.experimental.pallas import tpu as pltpu
from jax.sharding import PartitionSpec as P

MESH = pl.DeviceIdType.MESH
SLOT_COUNT = 3


def local_slots(expert_ids, experts):
    tokens, chosen = expert_ids.shape
    flat = expert_ids.reshape(tokens * chosen)
    onehot = (flat[:, None] == jnp.arange(experts, dtype=jnp.int32)[None, :]).astype(jnp.int32)
    before = jnp.cumsum(onehot, axis=0) - onehot
    return jnp.sum(before * onehot, axis=1).reshape(tokens, chosen)


def general_shards(
    expert_ids,
    route_weights,
    residual_grad,
    hidden_grad,
    gate_pre,
    up_pre,
    gate_weight,
    up_weight,
    attn_context,
    attn_grad,
):
    gate = gate_pre.astype(jnp.float32)
    upper = up_pre.astype(jnp.float32)
    grads = hidden_grad.astype(jnp.float32)
    sig = jax.nn.sigmoid(gate)
    up_term = (grads * gate * sig).astype(jnp.bfloat16)
    gate_term = (grads * upper * sig * (1.0 + gate * (1.0 - sig))).astype(jnp.bfloat16)
    rows_out = jnp.einsum(
        "brh,bdh->brd", gate_term, gate_weight, preferred_element_type=jnp.float32
    )
    rows_out = rows_out + jnp.einsum(
        "brh,bdh->brd", up_term, up_weight, preferred_element_type=jnp.float32
    )
    rows_out = rows_out.astype(jnp.bfloat16)
    received = lax.all_to_all(rows_out, "ep", split_axis=1, concat_axis=0, tiled=True)
    all_blocks, capacity, columns = received.shape
    received = received.reshape(all_blocks * capacity, columns).astype(jnp.float32)
    experts = all_blocks // 2
    slots = local_slots(expert_ids, experts)
    lower_col = 2 * expert_ids * capacity + slots
    upper_col = lower_col + capacity
    col_ids = jnp.arange(all_blocks * capacity, dtype=jnp.int32)[None, None, :]
    picks = (col_ids == lower_col[:, :, None]).astype(jnp.float32) + (
        col_ids == upper_col[:, :, None]
    ).astype(jnp.float32)
    combine = jnp.sum(route_weights[:, :, None] * picks, axis=1)
    gathered_sum = jnp.dot(combine, received, precision=lax.Precision.HIGHEST)
    input_grad = (residual_grad.astype(jnp.float32) + gathered_sum).astype(jnp.bfloat16)
    context_all = lax.all_gather(attn_context, "fsdp", axis=0, tiled=True)
    grad_all = lax.all_to_all(attn_grad, "fsdp", split_axis=1, concat_axis=0, tiled=True)
    proj_weight_grad = jnp.einsum(
        "ti,tj->ij", context_all, grad_all, preferred_element_type=jnp.float32
    )
    return (input_grad, proj_weight_grad)


def kernel(
    n_ep,
    ids_ref,
    route_ref,
    residual_ref,
    hidden_hbm,
    gate_hbm,
    up_hbm,
    gate_weight_hbm,
    up_weight_hbm,
    context_hbm,
    grad_hbm,
    input_grad_ref,
    proj_hbm,
    hidden_buf,
    gate_buf,
    up_buf,
    gate_weight_buf,
    up_weight_buf,
    gate_term,
    up_term,
    half_rows,
    rows_out,
    rows_in,
    context_all,
    grad_all,
    total,
    load_sem,
    own_sem,
    store_sem,
    context_send,
    context_recv,
    grad_send,
    grad_recv,
    rows_send,
    rows_recv,
):
    f32, bf16 = jnp.float32, jnp.bfloat16
    blocks, slots, hidden = hidden_hbm.shape
    columns = gate_weight_hbm.shape[1]
    tokens, context_cols = context_hbm.shape
    cap = slots // n_ep
    quarter = tokens // n_ep
    half = tokens // 2

    f = lax.axis_index("fsdp")
    z = lax.axis_index("ep")
    core, x, y = f % 2, (f // 2) % 2, f // 4

    def at(yy, xx, cc):
        return yy * 4 + xx * 2 + cc

    sib = at(y, x, 1 - core)
    x_same, x_other = at(y, 1 - x, core), at(y, 1 - x, 1 - core)
    y_same, y_other = at(1 - y, x, core), at(1 - y, x, 1 - core)
    d_same, d_other = at(1 - y, 1 - x, core), at(1 - y, 1 - x, 1 - core)
    own_chip, x_chip, y_chip, d_chip = f // 2, x_same // 2, y_same // 2, d_same // 2

    sources = (gate_weight_hbm, up_weight_hbm, hidden_hbm, gate_hbm, up_hbm)
    buffers = (gate_weight_buf, up_weight_buf, hidden_buf, gate_buf, up_buf)

    def loads(block):
        slot = block % SLOT_COUNT
        return [
            pltpu.make_async_copy(src.at[block], buf.at[slot], load_sem.at[i, slot])
            for i, (src, buf) in enumerate(zip(sources, buffers))
        ]

    for block in range(SLOT_COUNT - 1):
        for copy in loads(block):
            copy.start()

    def grad_columns(who):
        return pl.ds(pl.multiple_of(who * columns, 128), columns)

    own_copies = [
        pltpu.make_async_copy(context_hbm, context_all.at[f], own_sem.at[0]),
        pltpu.make_async_copy(grad_hbm.at[:, grad_columns(f)], grad_all.at[f], own_sem.at[1]),
    ]
    for copy in own_copies:
        copy.start()

    def remote(src, dst, send, recv, i, to):
        return pltpu.make_async_remote_copy(
            src_ref=src,
            dst_ref=dst,
            send_sem=send.at[i],
            recv_sem=recv.at[i],
            device_id=to,
            device_id_type=MESH,
        )

    first, second = pl.ds(0, half), pl.ds(half, half)
    context_moves = (
        (context_hbm, context_all.at[f], sib),
        (context_hbm, context_all.at[f], x_same),
        (context_hbm, context_all.at[f], y_same),
        (context_all.at[x_same, first], context_all.at[x_same, first], y_same),
        (context_all.at[y_same, second], context_all.at[y_same, second], x_same),
        (context_all.at[x_same], context_all.at[x_same], sib),
        (context_all.at[y_same], context_all.at[y_same], sib),
        (context_all.at[d_same, first], context_all.at[d_same, first], sib),
        (context_all.at[d_same, second], context_all.at[d_same, second], sib),
    )
    context_lands = (
        context_all.at[sib],
        context_all.at[x_same],
        context_all.at[y_same],
        context_all.at[d_same, first],
        context_all.at[d_same, second],
        context_all.at[x_other],
        context_all.at[y_other],
        context_all.at[d_other, first],
        context_all.at[d_other, second],
    )

    def context_out(i):
        src, dst, to = context_moves[i]
        return remote(src, dst, context_send, context_recv, i, (to, z))

    def context_in(i):
        land = context_lands[i]
        return remote(land, land, context_send, context_recv, i, (context_moves[i][2], z))

    def share(who):
        return pl.ds(pl.multiple_of(who * quarter, quarter), quarter)

    pair = pl.ds(2 * d_chip, 2)
    grad_targets = (sib, x_same, x_other, y_same, y_other, d_same, d_other)

    def grad_out(i):
        if i < 5:
            to = grad_targets[i]
            src, dst = grad_hbm.at[:, grad_columns(to)], grad_all.at[f]
        elif i < 7:
            to = grad_targets[i]
            src, dst = grad_hbm.at[share(z), grad_columns(to)], grad_all.at[f, share(z)]
        else:
            src = dst = grad_all.at[pair, share(z)]
            return remote(src, dst, grad_send, grad_recv, i, (f, (z + i - 6) % n_ep))
        return remote(src, dst, grad_send, grad_recv, i, (to, z))

    def grad_in(i):
        if i < 5:
            land, to = grad_all.at[grad_targets[i]], (grad_targets[i], z)
        elif i < 7:
            land, to = grad_all.at[grad_targets[i], share(z)], (grad_targets[i], z)
        else:
            from_z = (z + n_ep - (i - 6)) % n_ep
            land, to = grad_all.at[pair, share(from_z)], (f, from_z)
        return remote(land, land, grad_send, grad_recv, i, to)

    def rows_move(k):
        to = (z + k) % n_ep
        return remote(rows_out.at[to], rows_in.at[z], rows_send, rows_recv, k - 1, (f, to))

    def rows_land(k):
        source = (z + n_ep - k) % n_ep
        land = rows_in.at[source]
        return remote(land, land, rows_send, rows_recv, k - 1, (f, source))

    barrier = pltpu.get_barrier_semaphore()
    peers = [(who, z) for who in grad_targets] + [(f, (z + k) % n_ep) for k in range(1, n_ep)]
    for who in peers:
        pl.semaphore_signal(barrier, inc=1, device_id=who, device_id_type=MESH)
    pl.semaphore_wait(barrier, len(peers))

    for i in (1, 2, 0):
        context_out(i).start()
    for i in (5, 6, 0):
        grad_out(i).start()

    chunk = hidden // 7 if hidden % (7 * 128) == 0 else hidden

    def expert_step(block, carry):
        slot = block % SLOT_COUNT

        @pl.when(block + (SLOT_COUNT - 1) < blocks)
        def _():
            for copy in loads(block + (SLOT_COUNT - 1)):
                copy.start()

        @pl.when(block == 2)
        def _():
            for i in (1, 3, 2, 4):
                grad_out(i).start()

        @pl.when(block == blocks - 2)
        def _():
            context_in(1).wait_recv()
            context_out(3).start()
            context_out(5).start()
            context_in(2).wait_recv()
            context_out(4).start()
            context_out(6).start()
            grad_in(5).wait_recv()
            grad_in(6).wait_recv()
            for i in (7, 8, 9):
                grad_out(i).start()

        for copy in loads(block):
            copy.wait()
        for start in range(0, hidden, chunk):
            cols = pl.ds(start, chunk)
            grads = hidden_buf[slot, :, cols].astype(f32)
            gate = gate_buf[slot, :, cols].astype(f32)
            upper = up_buf[slot, :, cols].astype(f32)
            sig = 1.0 / (1.0 + jnp.exp(-gate))
            scaled = grads * sig
            up_term[:, cols] = (scaled * gate).astype(bf16)
            gate_term[:, cols] = (scaled * upper * (1.0 + gate * (1.0 - sig))).astype(bf16)
        dims = (((1,), (1,)), ((), ()))
        part = lax.dot_general(
            gate_term[...], gate_weight_buf[slot], dims, preferred_element_type=f32
        )
        part = part + lax.dot_general(
            up_term[...], up_weight_buf[slot], dims, preferred_element_type=f32
        )

        @pl.when(block % 2 == 0)
        def _():
            half_rows[...] = part

        @pl.when(block % 2 == 1)
        def _():
            both = (half_rows[...] + part).astype(bf16)
            for dest in range(n_ep):
                rows_out[dest, block // 2] = both[dest * cap : (dest + 1) * cap]

        return carry

    lax.fori_loop(0, blocks, expert_step, 0)

    for k in range(1, n_ep):
        rows_move(k).start()
    rows_in[z] = rows_out[z]

    step_cols = 256
    steps = context_cols // step_cols

    def store(i):
        rows = pl.ds(pl.multiple_of(i * step_cols, step_cols), step_cols)
        return pltpu.make_async_copy(total.at[rows], proj_hbm.at[rows], store_sem.at[i])

    def chip_product(chip, begin, end):
        def step(i, carry):
            cols = pl.ds(pl.multiple_of(i * step_cols, step_cols), step_cols)
            left = context_all[pl.ds(2 * chip, 2), :, cols].reshape(2 * tokens, step_cols)
            right = grad_all[pl.ds(2 * chip, 2)].reshape(2 * tokens, columns)
            product = lax.dot_general(
                left, right, (((0,), (0,)), ((), ())), preferred_element_type=f32
            )
            if begin:
                total[cols, :] = product
            else:
                total[cols, :] += product
            if end:
                store(i).start()
            return carry

        lax.fori_loop(0, steps, step, 0)

    for copy in own_copies:
        copy.wait()
    context_in(0).wait_recv()
    grad_in(0).wait_recv()
    chip_product(own_chip, True, False)

    routed, top = ids_ref.shape
    width = n_ep * (blocks // 2) * cap
    place = lax.broadcasted_iota(jnp.int32, (routed, width), 1)
    expert, row = place // cap, place % cap
    named = jnp.zeros((routed, width), f32)
    weight = jnp.zeros((routed, width), f32)
    for k in range(top):
        match = ids_ref[:, k : k + 1] == expert
        named = named + jnp.where(match, 1.0, 0.0)
        weight = weight + jnp.where(match, route_ref[:, k : k + 1], 0.0)
    earlier = lax.broadcasted_iota(jnp.int32, (routed, routed), 1) < lax.broadcasted_iota(
        jnp.int32, (routed, routed), 0
    )
    slot_of = jnp.dot(
        jnp.where(earlier, 1.0, 0.0).astype(bf16),
        named.astype(bf16),
        preferred_element_type=f32,
    )
    weight = jnp.where(slot_of == row.astype(f32), weight, 0.0)
    for k in range(1, n_ep):
        rows_land(k).wait_recv()
    received = rows_in[...].reshape(width, columns)
    result = residual_ref[...].astype(f32)
    for _ in range(3):
        piece = weight.astype(bf16)
        result = result + jnp.dot(piece, received, preferred_element_type=f32)
        weight = weight - piece.astype(f32)
    input_grad_ref[...] = result.astype(bf16)

    grad_in(1).wait_recv()
    grad_in(2).wait_recv()
    context_in(5).wait_recv()
    chip_product(x_chip, False, False)
    context_in(3).wait_recv()
    context_out(7).start()
    grad_in(3).wait_recv()
    grad_in(4).wait_recv()
    context_in(6).wait_recv()
    context_in(4).wait_recv()
    context_out(8).start()
    chip_product(y_chip, False, False)
    for i in (7, 8, 9):
        grad_in(i).wait_recv()
    context_in(7).wait_recv()
    context_in(8).wait_recv()
    chip_product(d_chip, False, True)

    for i in range(9):
        context_out(i).wait_send()
    for i in range(10):
        grad_out(i).wait_send()
    for k in range(1, n_ep):
        rows_move(k).wait_send()
    for i in range(steps):
        store(i).wait()


def kernel_shards(
    n_fsdp,
    n_ep,
    expert_ids,
    route_weights,
    residual_grad,
    hidden_grad,
    gate_pre,
    up_pre,
    gate_weight,
    up_weight,
    attn_context,
    attn_grad,
):
    blocks, slots, hidden = hidden_grad.shape
    columns = gate_weight.shape[1]
    tokens, context_cols = attn_context.shape
    cap = slots // n_ep
    bf16, f32 = jnp.bfloat16, jnp.float32
    vmem = pl.BlockSpec(memory_space=pltpu.VMEM)
    anywhere = pl.BlockSpec(memory_space=pl.ANY)
    dma = pltpu.SemaphoreType.DMA
    steps = context_cols // 256
    return pl.pallas_call(
        functools.partial(kernel, n_ep),
        out_shape=(
            jax.ShapeDtypeStruct(residual_grad.shape, bf16),
            jax.ShapeDtypeStruct((context_cols, columns), f32),
        ),
        in_specs=[vmem] * 3 + [anywhere] * 7,
        out_specs=(vmem, anywhere),
        scratch_shapes=[
            pltpu.VMEM((SLOT_COUNT, slots, hidden), bf16),
            pltpu.VMEM((SLOT_COUNT, slots, hidden), bf16),
            pltpu.VMEM((SLOT_COUNT, slots, hidden), bf16),
            pltpu.VMEM((SLOT_COUNT, columns, hidden), bf16),
            pltpu.VMEM((SLOT_COUNT, columns, hidden), bf16),
            pltpu.VMEM((slots, hidden), bf16),
            pltpu.VMEM((slots, hidden), bf16),
            pltpu.VMEM((slots, columns), f32),
            pltpu.VMEM((n_ep, blocks // 2, cap, columns), bf16),
            pltpu.VMEM((n_ep, blocks // 2, cap, columns), bf16),
            pltpu.VMEM((n_fsdp, tokens, context_cols), bf16),
            pltpu.VMEM((n_fsdp, tokens, columns), bf16),
            pltpu.VMEM((context_cols, columns), f32),
            dma((5, SLOT_COUNT)),
            dma((2,)),
            dma((steps,)),
            dma((9,)),
            dma((9,)),
            dma((10,)),
            dma((10,)),
            dma((n_ep - 1,)),
            dma((n_ep - 1,)),
        ],
        compiler_params=pltpu.CompilerParams(
            collective_id=0, has_side_effects=True, vmem_limit_bytes=58 * 1024 * 1024
        ),
        cost_estimate=pl.CostEstimate(
            flops=4 * blocks * slots * columns * hidden
            + 2 * n_fsdp * tokens * context_cols * columns,
            bytes_accessed=4 * blocks * columns * hidden + 6 * blocks * slots * hidden,
            transcendentals=blocks * slots * hidden,
        ),
        name="expert_and_projection",
    )(
        expert_ids,
        route_weights,
        residual_grad,
        hidden_grad,
        gate_pre,
        up_pre,
        gate_weight,
        up_weight,
        attn_context,
        attn_grad,
    )


def solution(mesh):
    n_fsdp, n_ep = mesh.shape["fsdp"], mesh.shape["ep"]

    def shards(*args):
        weight, context = args[6], args[8]
        fits = (
            n_fsdp == 8
            and n_ep == 4
            and weight.shape[1] % 128 == 0
            and context.shape[1] % 256 == 0
            and context.shape[0] % (16 * n_ep) == 0
            and args[3].shape[1] % (16 * n_ep) == 0
        )
        if fits:
            return kernel_shards(n_fsdp, n_ep, *args)
        return general_shards(*args)

    return jax.shard_map(
        shards,
        mesh=mesh,
        in_specs=(
            P("ep", None),
            P("ep", None),
            P("ep", "fsdp"),
            P("ep", None, None),
            P("ep", None, None),
            P("ep", None, None),
            P("ep", "fsdp", None),
            P("ep", "fsdp", None),
            P("fsdp", "ep"),
            P("fsdp", None),
        ),
        out_specs=(P("ep", "fsdp"), P("ep", "fsdp")),
        check_vma=False,
    )
```

```python
import functools

import jax
import jax.numpy as jnp
from jax import lax
from jax.experimental import pallas as pl
from jax.experimental.pallas import tpu as pltpu
from jax.sharding import PartitionSpec as P

MESH = pl.DeviceIdType.MESH
SLOT_COUNT = 3


def local_slots(expert_ids, experts):
    tokens, chosen = expert_ids.shape
    flat = expert_ids.reshape(tokens * chosen)
    onehot = (flat[:, None] == jnp.arange(experts, dtype=jnp.int32)[None, :]).astype(jnp.int32)
    before = jnp.cumsum(onehot, axis=0) - onehot
    return jnp.sum(before * onehot, axis=1).reshape(tokens, chosen)


def general_shards(
    expert_ids,
    route_weights,
    residual_grad,
    hidden_grad,
    gate_pre,
    up_pre,
    gate_weight,
    up_weight,
    attn_context,
    attn_grad,
):
    gate = gate_pre.astype(jnp.float32)
    upper = up_pre.astype(jnp.float32)
    grads = hidden_grad.astype(jnp.float32)
    sig = jax.nn.sigmoid(gate)
    up_term = (grads * gate * sig).astype(jnp.bfloat16)
    gate_term = (grads * upper * sig * (1.0 + gate * (1.0 - sig))).astype(jnp.bfloat16)
    rows_out = jnp.einsum(
        "brh,bdh->brd", gate_term, gate_weight, preferred_element_type=jnp.float32
    )
    rows_out = rows_out + jnp.einsum(
        "brh,bdh->brd", up_term, up_weight, preferred_element_type=jnp.float32
    )
    rows_out = rows_out.astype(jnp.bfloat16)
    received = lax.all_to_all(rows_out, "ep", split_axis=1, concat_axis=0, tiled=True)
    all_blocks, capacity, columns = received.shape
    received = received.reshape(all_blocks * capacity, columns).astype(jnp.float32)
    experts = all_blocks // 2
    slots = local_slots(expert_ids, experts)
    lower_col = 2 * expert_ids * capacity + slots
    upper_col = lower_col + capacity
    col_ids = jnp.arange(all_blocks * capacity, dtype=jnp.int32)[None, None, :]
    picks = (col_ids == lower_col[:, :, None]).astype(jnp.float32) + (
        col_ids == upper_col[:, :, None]
    ).astype(jnp.float32)
    combine = jnp.sum(route_weights[:, :, None] * picks, axis=1)
    gathered_sum = jnp.dot(combine, received, precision=lax.Precision.HIGHEST)
    input_grad = (residual_grad.astype(jnp.float32) + gathered_sum).astype(jnp.bfloat16)
    context_all = lax.all_gather(attn_context, "fsdp", axis=0, tiled=True)
    grad_all = lax.all_to_all(attn_grad, "fsdp", split_axis=1, concat_axis=0, tiled=True)
    proj_weight_grad = jnp.einsum(
        "ti,tj->ij", context_all, grad_all, preferred_element_type=jnp.float32
    )
    return (input_grad, proj_weight_grad)


def kernel(
    n_ep,
    ids_ref,
    route_ref,
    hidden_hbm,
    gate_hbm,
    up_hbm,
    gate_weight_hbm,
    up_weight_hbm,
    context_hbm,
    grad_hbm,
    gathered_ref,
    proj_hbm,
    far_context,
    far_grad,
    hidden_buf,
    gate_buf,
    up_buf,
    gate_weight_buf,
    up_weight_buf,
    gate_term,
    up_term,
    half_rows,
    rows_out,
    rows_in,
    context_all,
    grad_all,
    total,
    load_sem,
    own_sem,
    store_sem,
    context_send,
    context_recv,
    grad_send,
    grad_recv,
    rows_send,
    rows_recv,
):
    f32, bf16 = jnp.float32, jnp.bfloat16
    blocks, slots, hidden = hidden_hbm.shape
    columns = gate_weight_hbm.shape[1]
    tokens, context_cols = context_hbm.shape
    cap = slots // n_ep
    quarter = tokens // n_ep
    half = tokens // 2

    f = lax.axis_index("fsdp")
    z = lax.axis_index("ep")
    core, x, y = f % 2, (f // 2) % 2, f // 4

    def at(yy, xx, cc):
        return yy * 4 + xx * 2 + cc

    sib = at(y, x, 1 - core)
    x_same, x_other = at(y, 1 - x, core), at(y, 1 - x, 1 - core)
    y_same, y_other = at(1 - y, x, core), at(1 - y, x, 1 - core)
    d_same, d_other = at(1 - y, 1 - x, core), at(1 - y, 1 - x, 1 - core)
    own_chip, x_chip, y_chip = f // 2, x_same // 2, y_same // 2

    sources = (gate_weight_hbm, up_weight_hbm, hidden_hbm, gate_hbm, up_hbm)
    buffers = (gate_weight_buf, up_weight_buf, hidden_buf, gate_buf, up_buf)

    def loads(block):
        slot = block % SLOT_COUNT
        return [
            pltpu.make_async_copy(src.at[block], buf.at[slot], load_sem.at[i, slot])
            for i, (src, buf) in enumerate(zip(sources, buffers))
        ]

    for block in range(SLOT_COUNT - 1):
        for copy in loads(block):
            copy.start()

    def grad_columns(who):
        return pl.ds(pl.multiple_of(who * columns, 128), columns)

    own_copies = [
        pltpu.make_async_copy(context_hbm, context_all.at[f], own_sem.at[0]),
        pltpu.make_async_copy(grad_hbm.at[:, grad_columns(f)], grad_all.at[f], own_sem.at[1]),
    ]
    for copy in own_copies:
        copy.start()

    def remote(src, dst, send, recv, i, to):
        return pltpu.make_async_remote_copy(
            src_ref=src,
            dst_ref=dst,
            send_sem=send.at[i],
            recv_sem=recv.at[i],
            device_id=to,
            device_id_type=MESH,
        )

    first, second = pl.ds(0, half), pl.ds(half, half)
    context_moves = (
        (context_hbm, context_all.at[f], sib),
        (context_hbm, context_all.at[f], x_same),
        (context_hbm, context_all.at[f], y_same),
        (context_all.at[x_same, first], far_context.at[core, first], y_same),
        (context_all.at[y_same, second], far_context.at[core, second], x_same),
        (context_all.at[x_same], context_all.at[x_same], sib),
        (context_all.at[y_same], context_all.at[y_same], sib),
        (far_context.at[core, first], far_context.at[core, first], sib),
        (far_context.at[core, second], far_context.at[core, second], sib),
    )
    context_lands = (
        context_all.at[sib],
        context_all.at[x_same],
        context_all.at[y_same],
        far_context.at[core, first],
        far_context.at[core, second],
        context_all.at[x_other],
        context_all.at[y_other],
        far_context.at[1 - core, first],
        far_context.at[1 - core, second],
    )

    def context_out(i):
        src, dst, to = context_moves[i]
        return remote(src, dst, context_send, context_recv, i, (to, z))

    def context_in(i):
        land = context_lands[i]
        return remote(land, land, context_send, context_recv, i, (context_moves[i][2], z))

    def share(who):
        return pl.ds(pl.multiple_of(who * quarter, quarter), quarter)

    grad_targets = (sib, x_same, x_other, y_same, y_other, d_same, d_other)

    def grad_out(i):
        if i < 5:
            to = grad_targets[i]
            src, dst = grad_hbm.at[:, grad_columns(to)], grad_all.at[f]
        elif i < 7:
            to = grad_targets[i]
            src, dst = grad_hbm.at[share(z), grad_columns(to)], far_grad.at[core, share(z)]
        else:
            src = dst = far_grad.at[:, share(z)]
            return remote(src, dst, grad_send, grad_recv, i, (f, (z + i - 6) % n_ep))
        return remote(src, dst, grad_send, grad_recv, i, (to, z))

    def grad_in(i):
        if i < 5:
            land, to = grad_all.at[grad_targets[i]], (grad_targets[i], z)
        elif i < 7:
            land = far_grad.at[core if i == 5 else 1 - core, share(z)]
            to = (grad_targets[i], z)
        else:
            from_z = (z + n_ep - (i - 6)) % n_ep
            land, to = far_grad.at[:, share(from_z)], (f, from_z)
        return remote(land, land, grad_send, grad_recv, i, to)

    def rows_move(k):
        to = (z + k) % n_ep
        return remote(rows_out.at[to], rows_in.at[z], rows_send, rows_recv, k - 1, (f, to))

    def rows_land(k):
        source = (z + n_ep - k) % n_ep
        land = rows_in.at[source]
        return remote(land, land, rows_send, rows_recv, k - 1, (f, source))

    barrier = pltpu.get_barrier_semaphore()
    peers = [(who, z) for who in grad_targets] + [(f, (z + k) % n_ep) for k in range(1, n_ep)]
    for who in peers:
        pl.semaphore_signal(barrier, inc=1, device_id=who, device_id_type=MESH)
    pl.semaphore_wait(barrier, len(peers))

    for i in (1, 2, 0):
        context_out(i).start()
    for i in (5, 6, 0):
        grad_out(i).start()

    chunk = hidden // 7 if hidden % (7 * 128) == 0 else hidden

    def expert_step(block, carry):
        slot = block % SLOT_COUNT

        @pl.when(block + (SLOT_COUNT - 1) < blocks)
        def _():
            for copy in loads(block + (SLOT_COUNT - 1)):
                copy.start()

        @pl.when(block == 2)
        def _():
            for i in (1, 3, 2, 4):
                grad_out(i).start()

        @pl.when(block == blocks - 2)
        def _():
            context_in(1).wait_recv()
            context_out(3).start()
            context_out(5).start()
            context_in(2).wait_recv()
            context_out(4).start()
            context_out(6).start()
            grad_in(5).wait_recv()
            grad_in(6).wait_recv()
            for i in (7, 8, 9):
                grad_out(i).start()

        for copy in loads(block):
            copy.wait()
        for start in range(0, hidden, chunk):
            cols = pl.ds(start, chunk)
            grads = hidden_buf[slot, :, cols].astype(f32)
            gate = gate_buf[slot, :, cols].astype(f32)
            upper = up_buf[slot, :, cols].astype(f32)
            sig = 1.0 / (1.0 + jnp.exp(-gate))
            scaled = grads * sig
            up_term[:, cols] = (scaled * gate).astype(bf16)
            gate_term[:, cols] = (scaled * upper * (1.0 + gate * (1.0 - sig))).astype(bf16)
        dims = (((1,), (1,)), ((), ()))
        part = lax.dot_general(
            gate_weight_buf[slot], gate_term[...], dims, preferred_element_type=f32
        )
        part = part + lax.dot_general(
            up_weight_buf[slot], up_term[...], dims, preferred_element_type=f32
        )

        @pl.when(block % 2 == 0)
        def _():
            half_rows[...] = part

        @pl.when(block % 2 == 1)
        def _():
            both = (half_rows[...] + part).T.astype(bf16)
            for dest in range(n_ep):
                rows_out[dest, block // 2] = both[dest * cap : (dest + 1) * cap]

        return carry

    lax.fori_loop(0, blocks, expert_step, 0)

    for k in range(1, n_ep):
        rows_move(k).start()
    rows_in[z] = rows_out[z]

    step_cols = 256
    steps = context_cols // step_cols

    def store(i):
        rows = pl.ds(pl.multiple_of(i * step_cols, step_cols), step_cols)
        return pltpu.make_async_copy(total.at[rows], proj_hbm.at[rows], store_sem.at[i])

    def chip_product(chip, begin, end):
        def step(i, carry):
            cols = pl.ds(pl.multiple_of(i * step_cols, step_cols), step_cols)
            left = context_all[pl.ds(2 * chip, 2), :, cols].reshape(2 * tokens, step_cols)
            right = grad_all[pl.ds(2 * chip, 2)].reshape(2 * tokens, columns)
            product = lax.dot_general(
                left, right, (((0,), (0,)), ((), ())), preferred_element_type=f32
            )
            if begin:
                total[cols, :] = product
            else:
                total[cols, :] += product
            if end:
                store(i).start()
            return carry

        lax.fori_loop(0, steps, step, 0)

    for copy in own_copies:
        copy.wait()
    context_in(0).wait_recv()
    grad_in(0).wait_recv()
    chip_product(own_chip, True, False)

    top, routed = ids_ref.shape
    width = n_ep * (blocks // 2) * cap
    place = lax.broadcasted_iota(jnp.int32, (width, routed), 0)
    expert, row = place // cap, place % cap
    named = jnp.zeros((width, routed), f32)
    weight = jnp.zeros((width, routed), f32)
    for k in range(top):
        match = ids_ref[k : k + 1, :] == expert
        named = named + jnp.where(match, 1.0, 0.0)
        weight = weight + jnp.where(match, route_ref[k : k + 1, :], 0.0)
    earlier = lax.broadcasted_iota(jnp.int32, (routed, routed), 0) < lax.broadcasted_iota(
        jnp.int32, (routed, routed), 1
    )
    slot_of = jnp.dot(
        named.astype(bf16),
        jnp.where(earlier, 1.0, 0.0).astype(bf16),
        preferred_element_type=f32,
    )
    weight = jnp.where(slot_of == row.astype(f32), weight, 0.0)
    for k in range(1, n_ep):
        rows_land(k).wait_recv()
    received = rows_in[...].reshape(width, columns)
    gathered = jnp.zeros((routed, columns), f32)
    for _ in range(3):
        piece = weight.astype(bf16)
        gathered = gathered + lax.dot_general(
            piece, received, (((0,), (0,)), ((), ())), preferred_element_type=f32
        )
        weight = weight - piece.astype(f32)
    gathered_ref[...] = gathered

    grad_in(1).wait_recv()
    grad_in(2).wait_recv()
    context_in(5).wait_recv()
    chip_product(x_chip, False, False)
    context_in(3).wait_recv()
    context_out(7).start()
    grad_in(3).wait_recv()
    grad_in(4).wait_recv()
    context_in(6).wait_recv()
    context_in(4).wait_recv()
    context_out(8).start()
    chip_product(y_chip, False, True)
    for i in (7, 8, 9):
        grad_in(i).wait_recv()
    context_in(7).wait_recv()
    context_in(8).wait_recv()

    for i in range(9):
        context_out(i).wait_send()
    for i in range(10):
        grad_out(i).wait_send()
    for k in range(1, n_ep):
        rows_move(k).wait_send()
    for i in range(steps):
        store(i).wait()


def kernel_shards(
    n_fsdp,
    n_ep,
    expert_ids,
    route_weights,
    residual_grad,
    hidden_grad,
    gate_pre,
    up_pre,
    gate_weight,
    up_weight,
    attn_context,
    attn_grad,
):
    blocks, slots, hidden = hidden_grad.shape
    columns = gate_weight.shape[1]
    tokens, context_cols = attn_context.shape
    cap = slots // n_ep
    bf16, f32 = jnp.bfloat16, jnp.float32
    vmem = pl.BlockSpec(memory_space=pltpu.VMEM)
    anywhere = pl.BlockSpec(memory_space=pl.ANY)
    dma = pltpu.SemaphoreType.DMA
    steps = context_cols // 256
    gathered, near, far_context, far_grad = pl.pallas_call(
        functools.partial(kernel, n_ep),
        out_shape=(
            jax.ShapeDtypeStruct(residual_grad.shape, f32),
            jax.ShapeDtypeStruct((context_cols, columns), f32),
            jax.ShapeDtypeStruct((2, tokens, context_cols), bf16),
            jax.ShapeDtypeStruct((2, tokens, columns), bf16),
        ),
        in_specs=[vmem] * 2 + [anywhere] * 7,
        out_specs=(vmem, anywhere, anywhere, anywhere),
        scratch_shapes=[
            pltpu.VMEM((SLOT_COUNT, slots, hidden), bf16),
            pltpu.VMEM((SLOT_COUNT, slots, hidden), bf16),
            pltpu.VMEM((SLOT_COUNT, slots, hidden), bf16),
            pltpu.VMEM((SLOT_COUNT, columns, hidden), bf16),
            pltpu.VMEM((SLOT_COUNT, columns, hidden), bf16),
            pltpu.VMEM((slots, hidden), bf16),
            pltpu.VMEM((slots, hidden), bf16),
            pltpu.VMEM((columns, slots), f32),
            pltpu.VMEM((n_ep, blocks // 2, cap, columns), bf16),
            pltpu.VMEM((n_ep, blocks // 2, cap, columns), bf16),
            pltpu.VMEM((n_fsdp, tokens, context_cols), bf16),
            pltpu.VMEM((n_fsdp, tokens, columns), bf16),
            pltpu.VMEM((context_cols, columns), f32),
            dma((5, SLOT_COUNT)),
            dma((2,)),
            dma((steps,)),
            dma((9,)),
            dma((9,)),
            dma((10,)),
            dma((10,)),
            dma((n_ep - 1,)),
            dma((n_ep - 1,)),
        ],
        compiler_params=pltpu.CompilerParams(
            collective_id=0, has_side_effects=True, vmem_limit_bytes=58 * 1024 * 1024
        ),
        cost_estimate=pl.CostEstimate(
            flops=4 * blocks * slots * columns * hidden
            + 2 * n_fsdp * tokens * context_cols * columns,
            bytes_accessed=4 * blocks * columns * hidden + 6 * blocks * slots * hidden,
            transcendentals=blocks * slots * hidden,
        ),
        name="expert_and_projection",
    )(
        expert_ids.T,
        route_weights.T,
        hidden_grad,
        gate_pre,
        up_pre,
        gate_weight,
        up_weight,
        attn_context,
        attn_grad,
    )
    input_grad = (residual_grad.astype(f32) + gathered).astype(bf16)
    far = lax.dot_general(
        far_context.reshape(2 * tokens, context_cols),
        far_grad.reshape(2 * tokens, columns),
        (((0,), (0,)), ((), ())),
        preferred_element_type=f32,
    )
    return input_grad, near + far


def solution(mesh):
    n_fsdp, n_ep = mesh.shape["fsdp"], mesh.shape["ep"]

    def shards(*args):
        weight, context = args[6], args[8]
        fits = (
            n_fsdp == 8
            and n_ep == 4
            and weight.shape[1] % 128 == 0
            and context.shape[1] % 256 == 0
            and context.shape[0] % (16 * n_ep) == 0
            and args[3].shape[1] % (16 * n_ep) == 0
        )
        if fits:
            return kernel_shards(n_fsdp, n_ep, *args)
        return general_shards(*args)

    return jax.shard_map(
        shards,
        mesh=mesh,
        in_specs=(
            P("ep", None),
            P("ep", None),
            P("ep", "fsdp"),
            P("ep", None, None),
            P("ep", None, None),
            P("ep", None, None),
            P("ep", "fsdp", None),
            P("ep", "fsdp", None),
            P("fsdp", "ep"),
            P("fsdp", None),
        ),
        out_specs=(P("ep", "fsdp"), P("ep", "fsdp")),
        check_vma=False,
    )
```

```python
import functools

import jax
import jax.numpy as jnp
from jax import lax
from jax.experimental import pallas as pl
from jax.experimental.pallas import tpu as pltpu
from jax.sharding import PartitionSpec as P

MESH = pl.DeviceIdType.MESH
SLOT_COUNT = 3


def local_slots(expert_ids, experts):
    tokens, chosen = expert_ids.shape
    flat = expert_ids.reshape(tokens * chosen)
    onehot = (flat[:, None] == jnp.arange(experts, dtype=jnp.int32)[None, :]).astype(jnp.int32)
    before = jnp.cumsum(onehot, axis=0) - onehot
    return jnp.sum(before * onehot, axis=1).reshape(tokens, chosen)


def general_shards(
    expert_ids,
    route_weights,
    residual_grad,
    hidden_grad,
    gate_pre,
    up_pre,
    gate_weight,
    up_weight,
    attn_context,
    attn_grad,
):
    gate = gate_pre.astype(jnp.float32)
    upper = up_pre.astype(jnp.float32)
    grads = hidden_grad.astype(jnp.float32)
    sig = jax.nn.sigmoid(gate)
    up_term = (grads * gate * sig).astype(jnp.bfloat16)
    gate_term = (grads * upper * sig * (1.0 + gate * (1.0 - sig))).astype(jnp.bfloat16)
    rows_out = jnp.einsum(
        "brh,bdh->brd", gate_term, gate_weight, preferred_element_type=jnp.float32
    )
    rows_out = rows_out + jnp.einsum(
        "brh,bdh->brd", up_term, up_weight, preferred_element_type=jnp.float32
    )
    rows_out = rows_out.astype(jnp.bfloat16)
    received = lax.all_to_all(rows_out, "ep", split_axis=1, concat_axis=0, tiled=True)
    all_blocks, capacity, columns = received.shape
    received = received.reshape(all_blocks * capacity, columns).astype(jnp.float32)
    experts = all_blocks // 2
    slots = local_slots(expert_ids, experts)
    lower_col = 2 * expert_ids * capacity + slots
    upper_col = lower_col + capacity
    col_ids = jnp.arange(all_blocks * capacity, dtype=jnp.int32)[None, None, :]
    picks = (col_ids == lower_col[:, :, None]).astype(jnp.float32) + (
        col_ids == upper_col[:, :, None]
    ).astype(jnp.float32)
    combine = jnp.sum(route_weights[:, :, None] * picks, axis=1)
    gathered_sum = jnp.dot(combine, received, precision=lax.Precision.HIGHEST)
    input_grad = (residual_grad.astype(jnp.float32) + gathered_sum).astype(jnp.bfloat16)
    context_all = lax.all_gather(attn_context, "fsdp", axis=0, tiled=True)
    grad_all = lax.all_to_all(attn_grad, "fsdp", split_axis=1, concat_axis=0, tiled=True)
    proj_weight_grad = jnp.einsum(
        "ti,tj->ij", context_all, grad_all, preferred_element_type=jnp.float32
    )
    return (input_grad, proj_weight_grad)


def kernel(
    n_ep,
    ids_ref,
    route_ref,
    hidden_hbm,
    gate_hbm,
    up_hbm,
    gate_weight_hbm,
    up_weight_hbm,
    context_hbm,
    grad_hbm,
    gathered_ref,
    proj_hbm,
    far_context,
    far_grad,
    hidden_buf,
    gate_buf,
    up_buf,
    gate_weight_buf,
    up_weight_buf,
    gate_term,
    up_term,
    half_rows,
    rows_out,
    rows_in,
    context_all,
    grad_all,
    total,
    load_sem,
    own_sem,
    store_sem,
    context_send,
    context_recv,
    grad_send,
    grad_recv,
    rows_send,
    rows_recv,
):
    f32, bf16 = jnp.float32, jnp.bfloat16
    blocks, slots, hidden = hidden_hbm.shape
    columns = gate_weight_hbm.shape[1]
    tokens, context_cols = context_hbm.shape
    cap = slots // n_ep
    quarter = tokens // n_ep
    half = tokens // 2

    f = lax.axis_index("fsdp")
    z = lax.axis_index("ep")
    core, x, y = f % 2, (f // 2) % 2, f // 4

    def at(yy, xx, cc):
        return yy * 4 + xx * 2 + cc

    sib = at(y, x, 1 - core)
    x_same, x_other = at(y, 1 - x, core), at(y, 1 - x, 1 - core)
    y_same, y_other = at(1 - y, x, core), at(1 - y, x, 1 - core)
    d_same, d_other = at(1 - y, 1 - x, core), at(1 - y, 1 - x, 1 - core)
    own_chip, x_chip, y_chip = f // 2, x_same // 2, y_same // 2

    sources = (gate_weight_hbm, up_weight_hbm, hidden_hbm, gate_hbm, up_hbm)
    buffers = (gate_weight_buf, up_weight_buf, hidden_buf, gate_buf, up_buf)

    def loads(block):
        slot = block % SLOT_COUNT
        return [
            pltpu.make_async_copy(src.at[block], buf.at[slot], load_sem.at[i, slot])
            for i, (src, buf) in enumerate(zip(sources, buffers))
        ]

    for block in range(SLOT_COUNT - 1):
        for copy in loads(block):
            copy.start()

    def grad_columns(who):
        return pl.ds(pl.multiple_of(who * columns, 128), columns)

    own_copies = [
        pltpu.make_async_copy(context_hbm, context_all.at[f], own_sem.at[0]),
        pltpu.make_async_copy(grad_hbm.at[:, grad_columns(f)], grad_all.at[f], own_sem.at[1]),
    ]
    for copy in own_copies:
        copy.start()

    def remote(src, dst, send, recv, i, to):
        return pltpu.make_async_remote_copy(
            src_ref=src,
            dst_ref=dst,
            send_sem=send.at[i],
            recv_sem=recv.at[i],
            device_id=to,
            device_id_type=MESH,
        )

    first, second = pl.ds(0, half), pl.ds(half, half)
    context_moves = (
        (context_hbm, context_all.at[f], sib),
        (context_hbm, context_all.at[f], x_same),
        (context_hbm, context_all.at[f], y_same),
        (context_all.at[x_same, first], far_context.at[core, first], y_same),
        (context_all.at[y_same, second], far_context.at[core, second], x_same),
        (context_all.at[x_same], context_all.at[x_same], sib),
        (context_all.at[y_same], context_all.at[y_same], sib),
        (far_context.at[core, first], far_context.at[core, first], sib),
        (far_context.at[core, second], far_context.at[core, second], sib),
    )
    context_lands = (
        context_all.at[sib],
        context_all.at[x_same],
        context_all.at[y_same],
        far_context.at[core, first],
        far_context.at[core, second],
        context_all.at[x_other],
        context_all.at[y_other],
        far_context.at[1 - core, first],
        far_context.at[1 - core, second],
    )

    def context_out(i):
        src, dst, to = context_moves[i]
        return remote(src, dst, context_send, context_recv, i, (to, z))

    def context_in(i):
        land = context_lands[i]
        return remote(land, land, context_send, context_recv, i, (context_moves[i][2], z))

    def share(who):
        return pl.ds(pl.multiple_of(who * quarter, quarter), quarter)

    grad_targets = (sib, x_same, x_other, y_same, y_other, d_same, d_other)

    def grad_out(i):
        if i < 5:
            to = grad_targets[i]
            src, dst = grad_hbm.at[:, grad_columns(to)], grad_all.at[f]
        elif i < 7:
            to = grad_targets[i]
            src, dst = grad_hbm.at[share(z), grad_columns(to)], far_grad.at[core, share(z)]
        else:
            src = dst = far_grad.at[:, share(z)]
            return remote(src, dst, grad_send, grad_recv, i, (f, (z + i - 6) % n_ep))
        return remote(src, dst, grad_send, grad_recv, i, (to, z))

    def grad_in(i):
        if i < 5:
            land, to = grad_all.at[grad_targets[i]], (grad_targets[i], z)
        elif i < 7:
            land = far_grad.at[core if i == 5 else 1 - core, share(z)]
            to = (grad_targets[i], z)
        else:
            from_z = (z + n_ep - (i - 6)) % n_ep
            land, to = far_grad.at[:, share(from_z)], (f, from_z)
        return remote(land, land, grad_send, grad_recv, i, to)

    def rows_move(k):
        to = (z + k) % n_ep
        return remote(rows_out.at[to], rows_in.at[z], rows_send, rows_recv, k - 1, (f, to))

    def rows_land(k):
        source = (z + n_ep - k) % n_ep
        land = rows_in.at[source]
        return remote(land, land, rows_send, rows_recv, k - 1, (f, source))

    barrier = pltpu.get_barrier_semaphore()
    peers = [(who, z) for who in grad_targets] + [(f, (z + k) % n_ep) for k in range(1, n_ep)]
    for who in peers:
        pl.semaphore_signal(barrier, inc=1, device_id=who, device_id_type=MESH)
    pl.semaphore_wait(barrier, len(peers))

    for i in (5, 6):
        grad_out(i).start()
    for i in (1, 2, 0):
        context_out(i).start()
    grad_out(0).start()

    chunk = hidden // 7 if hidden % (7 * 128) == 0 else hidden

    def expert_step(block, carry):
        slot = block % SLOT_COUNT

        @pl.when(block + (SLOT_COUNT - 1) < blocks)
        def _():
            for copy in loads(block + (SLOT_COUNT - 1)):
                copy.start()

        @pl.when(block == 2)
        def _():
            for i in (1, 3, 2, 4):
                grad_out(i).start()

        @pl.when(block == 3)
        def _():
            grad_in(5).wait_recv()
            grad_in(6).wait_recv()
            for i in (7, 8, 9):
                grad_out(i).start()

        @pl.when(block == blocks - 2)
        def _():
            context_in(1).wait_recv()
            context_out(3).start()
            context_out(5).start()
            context_in(2).wait_recv()
            context_out(4).start()
            context_out(6).start()
        for copy in loads(block):
            copy.wait()
        for start in range(0, hidden, chunk):
            cols = pl.ds(start, chunk)
            grads = hidden_buf[slot, :, cols].astype(f32)
            gate = gate_buf[slot, :, cols].astype(f32)
            upper = up_buf[slot, :, cols].astype(f32)
            sig = 1.0 / (1.0 + jnp.exp(-gate))
            scaled = grads * sig
            up_term[:, cols] = (scaled * gate).astype(bf16)
            gate_term[:, cols] = (scaled * upper * (1.0 + gate * (1.0 - sig))).astype(bf16)
        dims = (((1,), (1,)), ((), ()))
        part = lax.dot_general(
            gate_weight_buf[slot], gate_term[...], dims, preferred_element_type=f32
        )
        part = part + lax.dot_general(
            up_weight_buf[slot], up_term[...], dims, preferred_element_type=f32
        )

        @pl.when(block % 2 == 0)
        def _():
            half_rows[...] = part

        @pl.when(block % 2 == 1)
        def _():
            both = (half_rows[...] + part).T.astype(bf16)
            for dest in range(n_ep):
                rows_out[dest, block // 2] = both[dest * cap : (dest + 1) * cap]

        return carry

    lax.fori_loop(0, blocks, expert_step, 0)

    for k in range(1, n_ep):
        rows_move(k).start()
    rows_in[z] = rows_out[z]

    step_cols = 256
    steps = context_cols // step_cols

    def store(i):
        rows = pl.ds(pl.multiple_of(i * step_cols, step_cols), step_cols)
        return pltpu.make_async_copy(total.at[rows], proj_hbm.at[rows], store_sem.at[i])

    def chip_product(chip, begin, end):
        def step(i, carry):
            cols = pl.ds(pl.multiple_of(i * step_cols, step_cols), step_cols)
            left = context_all[pl.ds(2 * chip, 2), :, cols].reshape(2 * tokens, step_cols)
            right = grad_all[pl.ds(2 * chip, 2)].reshape(2 * tokens, columns)
            product = lax.dot_general(
                left, right, (((0,), (0,)), ((), ())), preferred_element_type=f32
            )
            if begin:
                total[cols, :] = product
            else:
                total[cols, :] += product
            if end:
                store(i).start()
            return carry

        lax.fori_loop(0, steps, step, 0)

    for copy in own_copies:
        copy.wait()
    context_in(0).wait_recv()
    grad_in(0).wait_recv()
    chip_product(own_chip, True, False)

    top, routed = ids_ref.shape
    width = n_ep * (blocks // 2) * cap
    place = lax.broadcasted_iota(jnp.int32, (width, routed), 0)
    expert, row = place // cap, place % cap
    named = jnp.zeros((width, routed), f32)
    weight = jnp.zeros((width, routed), f32)
    for k in range(top):
        match = ids_ref[k : k + 1, :] == expert
        named = named + jnp.where(match, 1.0, 0.0)
        weight = weight + jnp.where(match, route_ref[k : k + 1, :], 0.0)
    earlier = lax.broadcasted_iota(jnp.int32, (routed, routed), 0) < lax.broadcasted_iota(
        jnp.int32, (routed, routed), 1
    )
    slot_of = jnp.dot(
        named.astype(bf16),
        jnp.where(earlier, 1.0, 0.0).astype(bf16),
        preferred_element_type=f32,
    )
    weight = jnp.where(slot_of == row.astype(f32), weight, 0.0)
    for k in range(1, n_ep):
        rows_land(k).wait_recv()
    received = rows_in[...].reshape(width, columns)
    gathered = jnp.zeros((routed, columns), f32)
    for _ in range(3):
        piece = weight.astype(bf16)
        gathered = gathered + lax.dot_general(
            piece, received, (((0,), (0,)), ((), ())), preferred_element_type=f32
        )
        weight = weight - piece.astype(f32)
    gathered_ref[...] = gathered

    grad_in(1).wait_recv()
    grad_in(2).wait_recv()
    context_in(5).wait_recv()
    chip_product(x_chip, False, False)
    context_in(3).wait_recv()
    context_out(7).start()
    grad_in(3).wait_recv()
    grad_in(4).wait_recv()
    context_in(6).wait_recv()
    context_in(4).wait_recv()
    context_out(8).start()
    chip_product(y_chip, False, True)
    for i in (7, 8, 9):
        grad_in(i).wait_recv()
    context_in(7).wait_recv()
    context_in(8).wait_recv()

    for i in range(9):
        context_out(i).wait_send()
    for i in range(10):
        grad_out(i).wait_send()
    for k in range(1, n_ep):
        rows_move(k).wait_send()
    for i in range(steps):
        store(i).wait()


def finish(residual_ref, gathered_ref, near_ref, context_ref, grad_ref, input_grad_ref, proj_ref):
    @pl.when(pl.program_id(0) == 0)
    def _():
        result = residual_ref[...].astype(jnp.float32) + gathered_ref[...]
        input_grad_ref[...] = result.astype(jnp.bfloat16)

    pair, tokens, cols = context_ref.shape
    left = context_ref[...].reshape(pair * tokens, cols)
    right = grad_ref[...].reshape(pair * tokens, grad_ref.shape[2])
    proj_ref[...] = near_ref[...] + lax.dot_general(
        left, right, (((0,), (0,)), ((), ())), preferred_element_type=jnp.float32
    )


def kernel_shards(
    n_fsdp,
    n_ep,
    expert_ids,
    route_weights,
    residual_grad,
    hidden_grad,
    gate_pre,
    up_pre,
    gate_weight,
    up_weight,
    attn_context,
    attn_grad,
):
    blocks, slots, hidden = hidden_grad.shape
    columns = gate_weight.shape[1]
    tokens, context_cols = attn_context.shape
    cap = slots // n_ep
    bf16, f32 = jnp.bfloat16, jnp.float32
    vmem = pl.BlockSpec(memory_space=pltpu.VMEM)
    anywhere = pl.BlockSpec(memory_space=pl.ANY)
    dma = pltpu.SemaphoreType.DMA
    steps = context_cols // 256
    gathered, near, far_context, far_grad = pl.pallas_call(
        functools.partial(kernel, n_ep),
        out_shape=(
            jax.ShapeDtypeStruct(residual_grad.shape, f32),
            jax.ShapeDtypeStruct((context_cols, columns), f32),
            jax.ShapeDtypeStruct((2, tokens, context_cols), bf16),
            jax.ShapeDtypeStruct((2, tokens, columns), bf16),
        ),
        in_specs=[vmem] * 2 + [anywhere] * 7,
        out_specs=(vmem, anywhere, anywhere, anywhere),
        scratch_shapes=[
            pltpu.VMEM((SLOT_COUNT, slots, hidden), bf16),
            pltpu.VMEM((SLOT_COUNT, slots, hidden), bf16),
            pltpu.VMEM((SLOT_COUNT, slots, hidden), bf16),
            pltpu.VMEM((SLOT_COUNT, columns, hidden), bf16),
            pltpu.VMEM((SLOT_COUNT, columns, hidden), bf16),
            pltpu.VMEM((slots, hidden), bf16),
            pltpu.VMEM((slots, hidden), bf16),
            pltpu.VMEM((columns, slots), f32),
            pltpu.VMEM((n_ep, blocks // 2, cap, columns), bf16),
            pltpu.VMEM((n_ep, blocks // 2, cap, columns), bf16),
            pltpu.VMEM((n_fsdp, tokens, context_cols), bf16),
            pltpu.VMEM((n_fsdp, tokens, columns), bf16),
            pltpu.VMEM((context_cols, columns), f32),
            dma((5, SLOT_COUNT)),
            dma((2,)),
            dma((steps,)),
            dma((9,)),
            dma((9,)),
            dma((10,)),
            dma((10,)),
            dma((n_ep - 1,)),
            dma((n_ep - 1,)),
        ],
        compiler_params=pltpu.CompilerParams(
            collective_id=0, has_side_effects=True, vmem_limit_bytes=58 * 1024 * 1024
        ),
        cost_estimate=pl.CostEstimate(
            flops=4 * blocks * slots * columns * hidden
            + 2 * n_fsdp * tokens * context_cols * columns,
            bytes_accessed=4 * blocks * columns * hidden + 6 * blocks * slots * hidden,
            transcendentals=blocks * slots * hidden,
        ),
        name="expert_and_projection",
    )(
        expert_ids.T,
        route_weights.T,
        hidden_grad,
        gate_pre,
        up_pre,
        gate_weight,
        up_weight,
        attn_context,
        attn_grad,
    )
    return pl.pallas_call(
        finish,
        grid=(steps,),
        out_shape=(
            jax.ShapeDtypeStruct(residual_grad.shape, bf16),
            jax.ShapeDtypeStruct((context_cols, columns), f32),
        ),
        in_specs=[
            pl.BlockSpec(residual_grad.shape, lambda i: (0, 0)),
            pl.BlockSpec(residual_grad.shape, lambda i: (0, 0)),
            pl.BlockSpec((256, columns), lambda i: (i, 0)),
            pl.BlockSpec((2, tokens, 256), lambda i: (0, 0, i)),
            pl.BlockSpec((2, tokens, columns), lambda i: (0, 0, 0)),
        ],
        out_specs=(
            pl.BlockSpec(residual_grad.shape, lambda i: (0, 0)),
            pl.BlockSpec((256, columns), lambda i: (i, 0)),
        ),
        compiler_params=pltpu.CompilerParams(vmem_limit_bytes=60 * 1024 * 1024),
        name="far_product",
    )(residual_grad, gathered, near, far_context, far_grad)


def solution(mesh):
    n_fsdp, n_ep = mesh.shape["fsdp"], mesh.shape["ep"]

    def shards(*args):
        weight, context = args[6], args[8]
        fits = (
            n_fsdp == 8
            and n_ep == 4
            and weight.shape[1] % 128 == 0
            and context.shape[1] % 256 == 0
            and context.shape[0] % (16 * n_ep) == 0
            and args[3].shape[1] % (16 * n_ep) == 0
        )
        if fits:
            return kernel_shards(n_fsdp, n_ep, *args)
        return general_shards(*args)

    return jax.shard_map(
        shards,
        mesh=mesh,
        in_specs=(
            P("ep", None),
            P("ep", None),
            P("ep", "fsdp"),
            P("ep", None, None),
            P("ep", None, None),
            P("ep", None, None),
            P("ep", "fsdp", None),
            P("ep", "fsdp", None),
            P("fsdp", "ep"),
            P("fsdp", None),
        ),
        out_specs=(P("ep", "fsdp"), P("ep", "fsdp")),
        check_vma=False,
    )
```
